512 devices in a mesh: node: 16 (over y, z_lo), cross: 32 (over z_hi, x, core).
Axes of the slice: x: 4, y: 8, z: 8 (z_hi: 4, z_lo: 2; z = z_hi * 2 + z_lo), core: 2. Of those that a mesh axis runs over, the one named last changes fastest.
Arguments:
- tokens: bfloat16 [4096, 5120], P('node', 'cross'), may hold values from -6 to 6
- weight_codes: int32 [5120, 20480], P('node', 'cross'), may hold values from -127 to 127
- weight_scales: float32 [5120, 160], P('node', 'cross'), may hold values from 5e-05 to 0.0004
- cotangent: bfloat16 [4096, 20480], P('node', 'cross'), may hold values from -6 to 6
- grad_exponents: int32 [5120, 160], P('node', 'cross'), may hold values from 6 to 9
Outputs:
- projected: bfloat16 [4096, 20480], P('node', 'cross')
- token_grad: bfloat16 [4096, 5120], P('node', 'cross')
- weight_grad: float32 [5120, 20480], P('node', 'cross')
The draws below stay inside these ranges and needn't reach their ends.
All inputs are finite; a program needn't handle non-finite values.
Results may differ from the reference program's by a relative error of at most 0.019.
Values may be sent and summed in bfloat16 or wider, within the bound.
A program may use at most 64 MiB of HBM per device.

```python
import math
import jax
import jax.numpy as jnp
from jax import lax

D = 5120
FW = 20480
QBLOCK = 128
TOK_DEV = 256
TOKENS = 4096
N_NODE = 16
N_CROSS = 32


def touch_ends(entries, own_key, smallest, top_value):
    spot = [jax.random.randint(jax.random.fold_in(own_key, axis), (), 0, length) for axis, length in enumerate(entries.shape)]
    longest = entries.shape.index(max(entries.shape))
    neighbour = spot[:longest] + [(spot[longest] + 1) % entries.shape[longest]] + spot[longest + 1:]
    return entries.at[tuple(spot)].set(smallest).at[tuple(neighbour)].set(top_value)


def with_spikes(result, own_key, source, target, blocks, factor):
    owner, partner = [(jnp.arange(result.shape[axis_at]) // (result.shape[axis_at] // blocks)).reshape([-1 if axis == axis_at else 1 for axis in range(result.ndim)]) for axis_at in (source, target)]
    chosen = jax.random.permutation(own_key, blocks)[partner]
    strong = (owner == chosen) | (owner == (partner + blocks // 2) % blocks)
    return jnp.where(strong, factor * result, result)


def shard_levels(own_key, extent, pieces, low, largest):
    loudness = 1.0
    for position, shards_of in pieces:
        steps = jax.random.uniform(jax.random.fold_in(jax.random.fold_in(own_key, 6), position), (shards_of,), jnp.float32, low / len(pieces), largest / len(pieces))
        loudness = loudness * jnp.repeat(jnp.exp(steps), extent[position] // shards_of).reshape((-1,) + (1,) * (len(extent) - 1 - position))
    return loudness


def normal_values(own_key, shape, deviation, bound, cuts=(), kind=jnp.bfloat16):
    values = deviation * jax.random.normal(own_key, shape, jnp.float32)
    if cuts:
        values = values * shard_levels(own_key, shape, cuts, -0.22, 0.18)
    return jnp.clip(values, -bound, bound).astype(kind)


def bell_draw_with(stream_key, dims, scale, most, split, heavy, kind=jnp.bfloat16):
    result = scale * jax.random.normal(stream_key, dims, jnp.float32)
    if split:
        result = result * shard_levels(stream_key, dims, split, -0.22, 0.18)
    return jnp.clip(with_spikes(result, jax.random.fold_in(stream_key, 3), *heavy), -most, most).astype(kind)


def setup_inputs(seed: int = 0) -> dict:
    keys = jax.random.split(jax.random.key(seed), 6)
    tokens = bell_draw_with(keys[0], (TOKENS, D), 1.0, 6.0, ((0, 16), (1, 32)), (0, 1, 32, 2.75))
    weight_codes = touch_ends(jax.random.randint(keys[1], (D, FW), -127, 128), jax.random.fold_in(keys[1], 1), -127, 127).astype(jnp.int32)
    weight_scales = jnp.clip(jnp.exp(math.log(0.0004) - 2.0794415 * jax.random.uniform(keys[2], (D, FW // QBLOCK), jnp.float32) ** shard_levels(keys[2], (D, FW // QBLOCK), ((0, 16), (1, 32)), -0.2, 0.2)), 4.999999873689376e-05, 0.0004)
    cotangent = normal_values(keys[3], (TOKENS, FW), 1.0, 6.0, ((0, 16), (1, 32)))
    grad_exponents = touch_ends(jax.random.randint(keys[4], (D, FW // QBLOCK), 6, 10), jax.random.fold_in(keys[4], 1), 6, 9).astype(jnp.int32)
    return {"tokens": tokens, "weight_codes": weight_codes, "weight_scales": weight_scales, "cotangent": cotangent, "grad_exponents": grad_exponents}


def reference(tokens, weight_codes, weight_scales, cotangent, grad_exponents):
    weight = (weight_codes.astype(jnp.float32) * jnp.repeat(weight_scales, QBLOCK, axis=1)).astype(jnp.bfloat16)
    projected = jnp.dot(tokens, weight, preferred_element_type=jnp.float32).astype(jnp.bfloat16)
    width_cross = FW // N_CROSS

    def input_part(running, group):
        offset = (group * width_cross).astype(jnp.int32)
        cot_cols = lax.dynamic_slice_in_dim(cotangent, offset, width_cross, 1)
        weight_cols = lax.dynamic_slice_in_dim(weight, offset, width_cross, 1)
        term = lax.dot_general(cot_cols, weight_cols, (((1,), (1,)), ((), ())), preferred_element_type=jnp.float32).astype(jnp.bfloat16)
        term = lax.optimization_barrier(term)
        return running + term.astype(jnp.float32), None

    grad_in, _ = lax.scan(input_part, jnp.zeros((TOKENS, D), jnp.float32), jnp.arange(N_CROSS, dtype=jnp.int32))
    token_grad = grad_in.astype(jnp.bfloat16)

    def accumulate(running, shard):
        offset = (shard * TOK_DEV).astype(jnp.int32)
        left_rows = lax.dynamic_slice_in_dim(tokens, offset, TOK_DEV, 0)
        right_rows = lax.dynamic_slice_in_dim(cotangent, offset, TOK_DEV, 0)
        product = lax.dot_general(left_rows, right_rows, (((0,), (0,)), ((), ())), preferred_element_type=jnp.float32).astype(jnp.bfloat16)
        product = lax.optimization_barrier(product)
        return running + product.astype(jnp.float32), None

    grad_sum, _ = lax.scan(accumulate, jnp.zeros((D, FW), jnp.float32), jnp.arange(N_NODE, dtype=jnp.int32))
    factor = jnp.exp2(-jnp.repeat(grad_exponents, QBLOCK, axis=1).astype(jnp.float32))
    weight_grad = grad_sum * factor
    return projected, token_grad, weight_grad
```

```python
import jax
import jax.numpy as jnp
from jax import lax
from jax.experimental import pallas as pl
from jax.experimental.pallas import tpu as pltpu
from jax.sharding import PartitionSpec as P

QBLOCK = 128
NY, NZ, NX = 8, 4, 4
MESH = pl.DeviceIdType.MESH
F32, BF16 = jnp.float32, jnp.bfloat16


def kernel(
    tok_ref, code_ref, scale_ref, cot_ref, exp_ref,
    out_ref, tgrad_ref, wgrad_ref,
    wts, cot, feats, pad, piece, part, from_core, summed, from_x, reduced, from_z,
    final, home, prod, ring, wg_send, wg_recv,
    cot_s, cot_r, one_s, one_r, tz_s, tz_r, tx_s, tx_r, tk_s, tk_r,
    gk_s, gk_r, gx_s, gx_r, gz_s, gz_r, ring_s, ring_r,
):
    node, cross = lax.axis_index("node"), lax.axis_index("cross")
    y, zl = node // 2, node % 2
    zh, x, k = cross // 8, (cross // 2) % NX, cross % 2
    tokens, width = cot_ref.shape
    half = tokens // 2
    rows = code_ref.shape[0]
    own = tok_ref.shape[1]

    def at(y=y, zl=zl, zh=zh, x=x, k=k):
        return (y * 2 + zl, zh * 8 + x * 2 + k)

    up, down = at(y=(y + 1) % NY), at(y=(y + NY - 1) % NY)
    pair = at(zl=1 - zl)
    core = at(k=1 - k)
    zs = [at(zh=(zh + o) % NZ) for o in range(1, NZ)]
    xs = [at(x=(x + o) % NX) for o in range(1, NX)]
    held = 2 * zh + x // 2
    swap = at(y=held, zh=y // 2, x=2 * (y % 2) + x % 2)
    away = held != y

    def remote(src, dst, send, recv, device):
        return pltpu.make_async_remote_copy(
            src_ref=src, dst_ref=dst, send_sem=send, recv_sem=recv,
            device_id=device, device_id_type=MESH,
        )

    started = []

    def go(copy):
        copy.start()
        started.append(copy)

    own_rows = pl.ds(pl.multiple_of(zl * rows, 32), rows)
    other_rows = pl.ds(pl.multiple_of((1 - zl) * rows, 32), rows)
    pad[...] = jnp.zeros_like(pad)
    pad[:, :own] = tok_ref[...]
    piece[...] = pad[...].T[:own]
    for b in range(width // QBLOCK):
        cols = slice(b * QBLOCK, (b + 1) * QBLOCK)
        wts[own_rows, cols] = (
            code_ref[:, cols].astype(F32) * scale_ref[:, b : b + 1]
        ).astype(BF16)

    barrier = pltpu.get_barrier_semaphore()
    friends = [up, down, pair, core] + zs + xs
    for device in friends:
        pl.semaphore_signal(barrier, inc=1, device_id=device, device_id_type=MESH)

    @pl.when(away)
    def _():
        pl.semaphore_signal(barrier, inc=1, device_id=swap, device_id_type=MESH)

    pl.semaphore_wait(barrier, len(friends) + away.astype(jnp.int32))

    def spot(t, g):
        return feats.at[t, pl.ds(pl.multiple_of(g * own, 32), own)]

    held_g = 2 * (x % 2) + k
    to_held = remote(piece, spot(y, held_g), one_s.at[0], one_r.at[0], swap)

    @pl.when(away)
    def _():
        to_held.start()

    wsend = remote(wts.at[own_rows], wts.at[own_rows], one_s.at[1], one_r.at[1], pair)
    go(wsend)

    hs = [pl.ds(0, half), pl.ds(half, half)]
    ways = [(up, -1), (down, 1)]

    def cot_copy(way, h, s, first):
        device, sign = ways[way]
        t = (y + sign * s + NY) % NY
        src = cot_ref.at[hs[h]] if first else cot.at[t, hs[h]]
        return remote(src, cot.at[t, hs[h]], cot_s.at[way, h, s], cot_r.at[way, h, s], device)

    def cot_arrive(way, h, s):
        t = (y + ways[way][1] * (s + 1) + NY) % NY
        slot = cot.at[t, hs[h]]
        remote(slot, slot, cot_s.at[way, h, s], cot_r.at[way, h, s], up).wait_recv()

    for i in range(2):
        for way in range(2):
            go(cot_copy(way, (i + way) % 2, 0, True))
    cot[y] = cot_ref[...]

    def cot_step(i):
        s = i // 2
        for way in range(2):
            h = (i + way) % 2
            cot_arrive(way, h, s)
            if i < 5:
                go(cot_copy(way, h, s + 1, False))

    def dist(i):
        return (y + i + NY) % NY

    def tok_send_x(a):
        t = 2 * ((zh + a) % NZ) + x // 2
        for o in range(1, NX):
            go(remote(spot(t, held_g), spot(t, held_g), tx_s.at[a, o - 1], tx_r.at[a, o - 1], xs[o - 1]))

    def tok_send_core(t, xl):
        g = 2 * xl + k
        go(remote(spot(t, g), spot(t, g), tk_s.at[t, xl], tk_r.at[t, xl], core))

    def tok_held():
        @pl.when(away)
        def _():
            slot = spot(held, held_g)
            remote(slot, slot, one_s.at[0], one_r.at[0], swap).wait_recv()

        @pl.when(jnp.logical_not(away))
        def _():
            spot(held, held_g)[...] = piece[...]

        for o in range(1, NZ):
            go(remote(spot(held, held_g), spot(held, held_g), tz_s.at[o - 1], tz_r.at[o - 1], zs[o - 1]))
        tok_send_x(0)
        tok_send_core(held, x % 2)

    def tok_from_z(a):
        t = 2 * ((zh + a) % NZ) + x // 2
        slot = spot(t, held_g)
        remote(slot, slot, tz_s.at[NZ - a - 1], tz_r.at[NZ - a - 1], core).wait_recv()
        tok_send_x(a)
        tok_send_core(t, x % 2)

    def tok_from_x(a, o):
        there = (x + o) % NX
        t = 2 * ((zh + a) % NZ) + there // 2
        slot = spot(t, 2 * (there % 2) + k)
        remote(slot, slot, tx_s.at[a, NX - o - 1], tx_r.at[a, NX - o - 1], core).wait_recv()
        tok_send_core(t, there % 2)

    def tok_from_core():
        for t in range(NY):
            for xl in range(2):
                slot = spot(t, 2 * xl + 1 - k)
                remote(slot, slot, tk_s.at[t, xl], tk_r.at[t, xl], core).wait_recv()

    def tg_part(t):
        part[t] = lax.dot_general(
            wts[...], cot[t], (((1,), (1,)), ((), ())), preferred_element_type=F32
        ).astype(BF16)
        for xl in range(2):
            src = part.at[t, pl.ds(pl.multiple_of((2 * xl + 1 - k) * own, 32), own)]
            go(remote(src, from_core.at[t, xl], gk_s.at[t, xl], gk_r.at[t, xl], core))

    def tg_x_copy(t, xl):
        there = 2 * (t % 2) + xl
        o = (x - there + NX) % NX
        slot = lax.max(o - 1, 0)
        return there != x, remote(
            summed.at[t, xl], from_x.at[t // 2, slot], gx_s.at[t, xl],
            gx_r.at[t // 2, slot], at(x=there),
        )

    def tg_sum(t):
        for xl in range(2):
            slot = from_core.at[t, xl]
            remote(slot, slot, gk_s.at[t, xl], gk_r.at[t, xl], core).wait_recv()
            mine = part[t, pl.ds(pl.multiple_of((2 * xl + k) * own, 32), own)]
            summed[t, xl] = (mine.astype(F32) + slot[...].astype(F32)).astype(BF16)
            leaves, copy = tg_x_copy(t, xl)

            @pl.when(leaves)
            def _():
                copy.start()

    def tg_from_x(a):
        b = (zh + a) % NZ
        total = summed[2 * b + x // 2, x % 2].astype(F32)
        for o in range(NX - 1):
            slot = from_x.at[b, o]
            remote(slot, slot, gx_s.at[0, 0], gx_r.at[b, o], core).wait_recv()
            total += slot[...].astype(F32)
        reduced[a] = total.astype(BF16)
        if a:
            go(remote(reduced.at[a], from_z.at[a - 1], gz_s.at[a - 1], gz_r.at[a - 1], zs[a - 1]))

    tg_home = remote(final, home, one_s.at[2], one_r.at[2], swap)

    def tg_from_z():
        total = reduced[0].astype(F32)
        for o in range(NZ - 1):
            slot = from_z.at[o]
            remote(slot, slot, gz_s.at[o], gz_r.at[o], core).wait_recv()
            total += slot[...].astype(F32)
        final[...] = total.astype(BF16)

        @pl.when(away)
        def _():
            tg_home.start()

    def tg_end():
        @pl.when(away)
        def _():
            tg_home.wait_recv()

        @pl.when(jnp.logical_not(away))
        def _():
            home[...] = final[...]

        pad[:own] = home[...]
        tgrad_ref[...] = pad[...].T[:, :own]

    def product(t):
        prod[t] = lax.dot_general(
            feats[t], wts[...], (((0,), (0,)), ((), ())), preferred_element_type=F32
        )

    def ring_copy(way, i):
        s, h = i // 2, (i + way) % 2
        return remote(
            ring.at[way, i], ring.at[way, i + 2], ring_s.at[way, i], ring_r.at[way, i], ways[way][0]
        )

    def ring_goal(way, i):
        steps = (4 if i % 2 == 0 else 3) - i // 2
        return (y - ways[way][1] * steps + NY) % NY

    def ring_start(way, i):
        h = (i + way) % 2
        ring[way, i] = prod[ring_goal(way, i), hs[h]].astype(BF16)
        go(ring_copy(way, i))

    def ring_step(i):
        for way in range(2):
            h = (i + way) % 2
            slot = ring.at[way, i + 2]
            remote(slot, slot, ring_s.at[way, i], ring_r.at[way, i], core).wait_recv()
            if i < 5:
                slot[...] = (
                    slot[...].astype(F32) + prod[ring_goal(way, i + 2), hs[h]]
                ).astype(BF16)
                go(ring_copy(way, i + 2))

    def wg_half(which):
        total = jnp.zeros((rows, width), F32)
        for t in range(NY):
            total += jnp.dot(feats[t, which], cot[t], preferred_element_type=F32)
        return total

    wg_copy = remote(wg_send, wg_recv, one_s.at[3], one_r.at[3], pair)

    def wg_start():
        wg_send[...] = wg_half(other_rows).astype(BF16)
        go(wg_copy)

    def wg_own():
        wgrad_ref[...] = wg_half(own_rows)

    def wg_end():
        wg_copy.wait_recv()
        factor = jnp.exp2(-exp_ref[...].astype(F32))
        for b in range(width // QBLOCK):
            cols = slice(b * QBLOCK, (b + 1) * QBLOCK)
            wgrad_ref[:, cols] = (
                wgrad_ref[:, cols] + wg_recv[:, cols].astype(F32)
            ) * factor[:, b : b + 1]

    cot_step(0)
    tok_held()
    cot_step(1)
    remote(wts.at[other_rows], wts.at[other_rows], one_s.at[1], one_r.at[1], pair).wait_recv()
    for i in (0, 1, -1):
        tg_part(dist(i))
    for a in (1, 3, 2):
        tok_from_z(a)
    cot_step(2)
    for o in (1, 3, 2):
        tok_from_x(0, o)
    for i in (0, 1, -1):
        tg_sum(dist(i))
    cot_step(3)
    for i in (2, -2):
        tg_part(dist(i))
    for o in (1, 3, 2):
        tok_from_x(1, o)
    cot_step(4)
    for i in (2, -2):
        tg_sum(dist(i))
    for a in (3, 2):
        for o in (1, 3, 2):
            tok_from_x(a, o)
    cot_step(5)
    tok_from_core()
    product(dist(4))
    ring_start(0, 0)
    ring_start(1, 0)
    product(dist(3))
    ring_start(0, 1)
    product(dist(-3))
    ring_start(1, 1)
    for i in (3, -3):
        tg_part(dist(i))
    product(dist(2))
    product(dist(-2))
    cot_step(6)
    tg_part(dist(4))
    for i in (3, -3):
        tg_sum(dist(i))
    ring_step(0)
    tg_sum(dist(4))
    product(dist(1))
    product(dist(-1))
    ring_step(1)
    wg_start()
    ring_step(2)
    for a in (1, 2, 3, 0):
        tg_from_x(a)
    product(y)
    ring_step(3)
    wg_own()
    tg_from_z()
    ring_step(4)
    tg_end()
    wg_end()
    ring_step(5)
    ring_step(6)
    for h in range(2):
        out_ref[hs[h]] = (
            prod[y, hs[h]]
            + ring[0, 8 - h].astype(F32)
            + ring[1, 7 + h].astype(F32)
        ).astype(BF16)

    for copy in started:
        copy.wait_send()
    for t in range(NY):
        for xl in range(2):
            leaves, copy = tg_x_copy(t, xl)

            @pl.when(leaves)
            def _():
                copy.wait_send()

    @pl.when(away)
    def _():
        to_held.wait_send()
        tg_home.wait_send()


def on_device(tokens, weight_codes, weight_scales, cotangent, grad_exponents):
    count, own = tokens.shape
    rows, width = weight_codes.shape
    depth = 2 * rows
    dma = pltpu.SemaphoreType.DMA
    vmem = pl.BlockSpec(memory_space=pltpu.VMEM)
    scratch = [
        pltpu.VMEM((depth, width), BF16),
        pltpu.VMEM((NY, count, width), BF16),
        pltpu.VMEM((NY, depth, count), BF16),
        pltpu.VMEM((count, count), BF16),
        pltpu.VMEM((own, count), BF16),
        pltpu.VMEM((NY, depth, count), BF16),
        pltpu.VMEM((NY, 2, own, count), BF16),
        pltpu.VMEM((NY, 2, own, count), BF16),
        pltpu.VMEM((NZ, NX - 1, own, count), BF16),
        pltpu.VMEM((NZ, own, count), BF16),
        pltpu.VMEM((NZ - 1, own, count), BF16),
        pltpu.VMEM((own, count), BF16),
        pltpu.VMEM((own, count), BF16),
        pltpu.VMEM((NY, count, width), F32),
        pltpu.VMEM((2, 9, count // 2, width), BF16),
        pltpu.VMEM((rows, width), BF16),
        pltpu.VMEM((rows, width), BF16),
        dma((2, 2, 4)), dma((2, 2, 4)),
        dma((4,)), dma((4,)),
        dma((NZ - 1,)), dma((NZ - 1,)),
        dma((NZ, NX - 1)), dma((NZ, NX - 1)),
        dma((NY, 2)), dma((NY, 2)),
        dma((NY, 2)), dma((NY, 2)),
        dma((NY, 2)), dma((NZ, NX - 1)),
        dma((NZ - 1,)), dma((NZ - 1,)),
        dma((2, 7)), dma((2, 7)),
    ]
    return pl.pallas_call(
        kernel,
        name="up_projection",
        out_shape=(
            jax.ShapeDtypeStruct((count, width), BF16),
            jax.ShapeDtypeStruct((count, own), BF16),
            jax.ShapeDtypeStruct((rows, width), F32),
        ),
        in_specs=[vmem] * 5,
        out_specs=(vmem, vmem, vmem),
        scratch_shapes=scratch,
        compiler_params=pltpu.CompilerParams(
            collective_id=0, has_side_effects=True, vmem_limit_bytes=56 << 20
        ),
    )(tokens, weight_codes, weight_scales, cotangent, grad_exponents)


def solution(mesh):
    placed = P("node", "cross")
    return jax.shard_map(
        on_device,
        mesh=mesh,
        in_specs=(placed,) * 5,
        out_specs=(placed,) * 3,
        check_vma=False,
    )
```

```python
import jax
import jax.numpy as jnp
from jax import lax
from jax.experimental import pallas as pl
from jax.experimental.pallas import tpu as pltpu
from jax.sharding import PartitionSpec as P

QBLOCK = 128
VMEM = 40 << 20
NY, NZ, NX = 8, 4, 4
HERE = NY // 2
PARTS = 2
MESH = pl.DeviceIdType.MESH
F32, BF16 = jnp.float32, jnp.bfloat16


def kernel(
    tok_hbm, code_hbm, scale_hbm, cot_hbm, exp_hbm,
    out_ref, tgrad_ref, wgrad_ref,
    tok, code, scale, expo, wts, cot, feats, narrow, part, from_core, summed,
    from_x, reduced, from_z, final, home, prod, ring, wg_send, wg_recv,
    in_s, to_s, to_r, cot_s, cot_r, one_s, one_r, tz_s, tz_r, tx_s, tx_r, tk_s, tk_r,
    gk_s, gk_r, gx_s, gx_r, gz_s, gz_r, ring_s, ring_r,
):
    node, cross = lax.axis_index("node"), lax.axis_index("cross")
    y, zl = node // 2, node % 2
    zh, x, k = cross // 8, (cross // 2) % NX, cross % 2
    tokens, width = cot_hbm.shape
    half = tokens // 2
    rows = code_hbm.shape[0]
    own = tok_hbm.shape[0]

    own_slot = cot.at[HERE]
    loads = [
        pltpu.make_async_copy(src, dst, in_s.at[i])
        for i, (src, dst) in enumerate(
            [(tok_hbm, tok), (cot_hbm, own_slot), (code_hbm, code), (scale_hbm, scale), (exp_hbm, expo)]
        )
    ]
    for load in loads:
        load.start()

    def at(y=y, zl=zl, zh=zh, x=x, k=k):
        return (y * 2 + zl, zh * 8 + x * 2 + k)

    up, down = at(y=(y + 1) % NY), at(y=(y + NY - 1) % NY)
    pair = at(zl=1 - zl)
    core = at(k=1 - k)
    zs = [at(zh=(zh + o) % NZ) for o in range(1, NZ)]
    xs = [at(x=(x + o) % NX) for o in range(1, NX)]
    place = 2 * zh + x // 2
    slot_there = (y - place + HERE + NY) % NY
    owner = at(y=place, zh=slot_there // 2, x=2 * (slot_there % 2) + x % 2)
    home_of = at(y=(y + NY - HERE + place) % NY, zh=y // 2, x=2 * (y % 2) + x % 2)
    moves = jnp.logical_or(place != y, place != HERE)

    def remote(src, dst, send, recv, device):
        return pltpu.make_async_remote_copy(
            src_ref=src, dst_ref=dst, send_sem=send, recv_sem=recv,
            device_id=device, device_id_type=MESH,
        )

    def landed(slot, recv):
        remote(slot, slot, one_s.at[0], recv, core).wait_recv()

    started = []

    def go(copy):
        copy.start()
        started.append(copy)

    def columns(blocks):
        count = blocks.shape[0]
        narrow[...] = jnp.zeros_like(narrow)
        narrow[:count, :rows] = blocks
        return narrow[...].T[:rows, :count]

    barrier = pltpu.get_barrier_semaphore()
    friends = [up, down, pair, core] + zs + xs

    def greet(device):
        pl.semaphore_signal(barrier, inc=1, device_id=device, device_id_type=MESH)

    for device in friends:
        greet(device)

    @pl.when(moves)
    def _():
        greet(owner)
        greet(home_of)

    pl.semaphore_wait(barrier, len(friends) + 2 * moves.astype(jnp.int32))

    size = own // PARTS

    def spot(e, g, p=None):
        start = g * own if p is None else g * own + p * size
        return feats.at[e, pl.ds(pl.multiple_of(start, 16), own if p is None else size)]

    own_g = 2 * (x % 2) + k
    to_owner = [
        remote(tok.at[pl.ds(p * size, size)], spot(slot_there, own_g, p), to_s.at[p], to_r.at[p], owner)
        for p in range(PARTS)
    ]

    def tok_start():
        @pl.when(moves)
        def _():
            for copy in to_owner:
                copy.start()

        @pl.when(jnp.logical_not(moves))
        def _():
            spot(place, own_g)[...] = tok[...]

    def tok_send_x(j, p):
        src = spot(2 * j + x // 2, own_g, p)
        for o in (1, 3, 2):
            go(remote(src, src, tx_s.at[j, o - 1, p], tx_r.at[j, o - 1, p], xs[o - 1]))

    def tok_send_core(e, xl):
        src = spot(e, 2 * xl + k)
        go(remote(src, src, tk_s.at[e, xl], tk_r.at[e, xl], core))

    def tok_own():
        for p in range(PARTS):
            src = spot(place, own_g, p)

            @pl.when(moves)
            def _():
                landed(src, to_r.at[p])

            for o in range(1, NZ):
                go(remote(src, src, tz_s.at[o - 1, p], tz_r.at[zh, p], zs[o - 1]))
            tok_send_x(zh, p)
        tok_send_core(place, x % 2)

    need = [0, 3, 1, 2]
    ahead = (zh > 0).astype(jnp.int32) + (zh % 3 > 0).astype(jnp.int32) + (zh == 2).astype(jnp.int32)
    turn_of = [zh]
    for m in range(NZ - 1):
        later = (ahead <= m).astype(jnp.int32)
        turn_of.append(need[m] + later * (need[m + 1] - need[m]))

    def tok_from_z(m):
        j = turn_of[m]
        e = 2 * j + x // 2
        for p in range(PARTS):
            landed(spot(e, own_g, p), tz_r.at[j, p])
            tok_send_x(j, p)
        tok_send_core(e, x % 2)

    def tok_from_x(m):
        j = turn_of[m]
        for o in (1, 3, 2):
            there = (x + o) % NX
            e = 2 * j + there // 2
            for p in range(PARTS):
                landed(spot(e, 2 * (there % 2) + k, p), tx_r.at[j, NX - o - 1, p])
            tok_send_core(e, there % 2)

    def tok_from_core(e):
        for xl in range(2):
            landed(spot(e, 2 * xl + 1 - k), tk_r.at[e, xl])

    own_rows = pl.ds(pl.multiple_of(zl * rows, 32), rows)
    other_rows = pl.ds(pl.multiple_of((1 - zl) * rows, 32), rows)
    wsend = remote(wts.at[own_rows], wts.at[own_rows], one_s.at[1], one_r.at[1], pair)

    def weights_own():
        loads[2].wait()
        loads[3].wait()
        scales = columns(scale[...])
        for b in range(width // QBLOCK):
            cols = slice(b * QBLOCK, (b + 1) * QBLOCK)
            wts[own_rows, cols] = (
                code[:, cols].astype(F32) * scales[:, b : b + 1]
            ).astype(BF16)

    def weights_send():
        go(wsend)

    def weights_other():
        landed(wts.at[other_rows], one_r.at[1])

    hs = [pl.ds(0, half), pl.ds(half, half)]
    ways = [(up, -1), (down, 1)]

    def cot_slot(way, s):
        return (HERE + ways[way][1] * s + NY) % NY

    def cot_copy(way, h, s):
        return remote(
            cot.at[cot_slot(way, s), hs[h]], cot.at[cot_slot(way, s + 1), hs[h]],
            cot_s.at[way, h, s], cot_r.at[way, h, s], ways[way][0],
        )

    def cot_start():
        for i in range(2):
            for way in range(2):
                go(cot_copy(way, (i + way) % 2, 0))

    def cot_step(i):
        s = i // 2
        for way in range(2):
            h = (i + way) % 2
            landed(cot.at[cot_slot(way, s + 1), hs[h]], cot_r.at[way, h, s])
            if i < 5:
                go(cot_copy(way, h, s + 1))

    def tg_part(i):
        e = (HERE + i) % NY
        part[e] = lax.dot_general(
            wts[...], cot[e], (((1,), (1,)), ((), ())), preferred_element_type=F32
        ).astype(BF16)
        for xl in range(2):
            src = part.at[e, pl.ds(pl.multiple_of((2 * xl + 1 - k) * own, 32), own)]
            go(remote(src, from_core.at[e, xl], gk_s.at[e, xl], gk_r.at[e, xl], core))

    def tg_x_copy(e, xl):
        there = 2 * (e % 2) + xl
        o = (x - there + NX) % NX
        slot = lax.max(o - 1, 0)
        return there != x, remote(
            summed.at[e, xl], from_x.at[e // 2, slot], gx_s.at[e, xl],
            gx_r.at[e // 2, slot], at(x=there),
        )

    def tg_sum(i):
        e = (HERE + i) % NY
        for xl in range(2):
            slot = from_core.at[e, xl]
            landed(slot, gk_r.at[e, xl])
            mine = part[e, pl.ds(pl.multiple_of((2 * xl + k) * own, 32), own)]
            summed[e, xl] = (mine.astype(F32) + slot[...].astype(F32)).astype(BF16)
            leaves, copy = tg_x_copy(e, xl)

            @pl.when(leaves)
            def _():
                copy.start()

    def tg_z_copy(j):
        o = (zh - j + NZ) % NZ
        slot = lax.max(o - 1, 0)
        return j != zh, remote(
            reduced.at[j], from_z.at[slot], gz_s.at[j], gz_r.at[slot], at(zh=j)
        )

    def tg_from_x(j):
        total = summed[2 * j + x // 2, x % 2].astype(F32)
        for o in range(NX - 1):
            landed(from_x.at[j, o], gx_r.at[j, o])
            total += from_x[j, o].astype(F32)
        reduced[j] = total.astype(BF16)
        leaves, copy = tg_z_copy(j)

        @pl.when(leaves)
        def _():
            copy.start()

    to_home = remote(final, home, one_s.at[2], one_r.at[2], home_of)

    def tg_from_z():
        total = reduced[zh].astype(F32)
        for o in range(NZ - 1):
            landed(from_z.at[o], gz_r.at[o])
            total += from_z[o].astype(F32)
        final[...] = total.astype(BF16)

        @pl.when(moves)
        def _():
            to_home.start()

    def tg_end():
        @pl.when(moves)
        def _():
            to_home.wait_recv()
            tgrad_ref[...] = home[...]

        @pl.when(jnp.logical_not(moves))
        def _():
            tgrad_ref[...] = final[...]

    def product(i):
        e = (HERE + i) % NY
        prod[e] = lax.dot_general(
            feats[e], wts[...], (((0,), (0,)), ((), ())), preferred_element_type=F32
        )

    def ring_copy(way, i):
        return remote(
            ring.at[way, i], ring.at[way, i + 2], ring_s.at[way, i], ring_r.at[way, i], ways[way][0]
        )

    def ring_goal(way, i):
        steps = (4 if i % 2 == 0 else 3) - i // 2
        return (HERE - ways[way][1] * steps + NY) % NY

    def ring_start(way, i):
        h = (i + way) % 2
        ring[way, i] = prod[ring_goal(way, i), hs[h]].astype(BF16)
        go(ring_copy(way, i))

    def ring_step(i):
        for way in range(2):
            h = (i + way) % 2
            slot = ring.at[way, i + 2]
            landed(slot, ring_r.at[way, i])
            if i < 5:
                slot[...] = (
                    slot[...].astype(F32) + prod[ring_goal(way, i + 2), hs[h]]
                ).astype(BF16)
                go(ring_copy(way, i + 2))

    def wg_half(which):
        total = jnp.zeros((rows, width), F32)
        for e in range(NY):
            total += jnp.dot(feats[e, which], cot[e], preferred_element_type=F32)
        return total

    wg_copy = remote(wg_send, wg_recv, one_s.at[3], one_r.at[3], pair)

    def wg_start():
        wg_send[...] = wg_half(other_rows).astype(BF16)
        go(wg_copy)

    def wg_own():
        wgrad_ref[...] = wg_half(own_rows)

    def wg_end():
        wg_copy.wait_recv()
        factor = columns(jnp.exp2(-expo[...].astype(F32)))
        for b in range(width // QBLOCK):
            cols = slice(b * QBLOCK, (b + 1) * QBLOCK)
            wgrad_ref[:, cols] = (
                wgrad_ref[:, cols] + wg_recv[:, cols].astype(F32)
            ) * factor[:, b : b + 1]

    loads[0].wait()
    tok_start()
    loads[1].wait()
    cot_start()
    weights_own()
    weights_send()
    loads[4].wait()
    cot_step(0)
    tok_own()
    cot_step(1)
    tok_from_z(1)
    cot_step(2)
    tok_from_z(2)
    tok_from_x(0)
    tok_from_z(3)
    cot_step(3)
    weights_other()
    for i in (0, 1, -1):
        tg_part(i)
    tok_from_x(1)
    for i in (0, 1, -1):
        tg_sum(i)
    cot_step(4)
    for i in (2, -2):
        tg_part(i)
    tok_from_x(2)
    for e in (0, 1, 7):
        tok_from_core(e)
    product(4)
    ring_start(0, 0)
    ring_start(1, 0)
    product(3)
    ring_start(0, 1)
    product(-3)
    ring_start(1, 1)
    tok_from_x(3)
    for i in (2, -2):
        tg_sum(i)
    cot_step(5)
    for i in (3, -3):
        tg_part(i)
    cot_step(6)
    tg_part(4)
    for e in (6, 2):
        tok_from_core(e)
    product(2)
    product(-2)
    for i in (3, -3, 4):
        tg_sum(i)
    ring_step(0)
    for e in (5, 3, 4):
        tok_from_core(e)
    wg_start()
    tg_from_x(2)
    ring_step(1)
    product(1)
    product(-1)
    tg_from_x(1)
    tg_from_x(3)
    ring_step(2)
    tg_from_x(0)
    product(0)
    ring_step(3)
    tg_from_z()
    ring_step(4)
    wg_own()
    wg_end()
    ring_step(5)
    tg_end()
    ring_step(6)
    for h in range(2):
        out_ref[hs[h]] = (
            prod[HERE, hs[h]]
            + ring[0, 8 - h].astype(F32)
            + ring[1, 7 + h].astype(F32)
        ).astype(BF16)

    for copy in started:
        copy.wait_send()
    some = [tg_x_copy(e, xl) for e in range(NY) for xl in range(2)]
    some += [tg_z_copy(j) for j in range(NZ)]
    some += [(moves, copy) for copy in to_owner + [to_home]]
    for leaves, copy in some:

        @pl.when(leaves)
        def _():
            copy.wait_send()


def on_device(tokens, weight_codes, weight_scales, cotangent, grad_exponents):
    count, own = tokens.shape
    rows, width = weight_codes.shape
    depth = 2 * rows
    dma = pltpu.SemaphoreType.DMA
    vmem = pl.BlockSpec(memory_space=pltpu.VMEM)
    scratch = [
        pltpu.VMEM((own, count), BF16),
        pltpu.VMEM((rows, width), jnp.int32),
        pltpu.VMEM((width // QBLOCK, rows), F32),
        pltpu.VMEM((width // QBLOCK, rows), jnp.int32),
        pltpu.VMEM((depth, width), BF16),
        pltpu.VMEM((NY, count, width), BF16),
        pltpu.VMEM((NY, depth, count), BF16),
        pltpu.VMEM((8, -(-rows // 128) * 128), F32),
        pltpu.VMEM((NY, depth, count), BF16),
        pltpu.VMEM((NY, 2, own, count), BF16),
        pltpu.VMEM((NY, 2, own, count), BF16),
        pltpu.VMEM((NZ, NX - 1, own, count), BF16),
        pltpu.VMEM((NZ, own, count), BF16),
        pltpu.VMEM((NZ - 1, own, count), BF16),
        pltpu.VMEM((own, count), BF16),
        pltpu.VMEM((own, count), BF16),
        pltpu.VMEM((NY, count, width), F32),
        pltpu.VMEM((2, 9, count // 2, width), BF16),
        pltpu.VMEM((rows, width), BF16),
        pltpu.VMEM((rows, width), BF16),
        dma((5,)),
        dma((PARTS,)), dma((PARTS,)),
        dma((2, 2, 4)), dma((2, 2, 4)),
        dma((4,)), dma((4,)),
        dma((NZ - 1, PARTS)), dma((NZ, PARTS)),
        dma((NZ, NX - 1, PARTS)), dma((NZ, NX - 1, PARTS)),
        dma((NY, 2)), dma((NY, 2)),
        dma((NY, 2)), dma((NY, 2)),
        dma((NY, 2)), dma((NZ, NX - 1)),
        dma((NZ,)), dma((NZ - 1,)),
        dma((2, 7)), dma((2, 7)),
    ]
    projected, token_grad, weight_grad = pl.pallas_call(
        kernel,
        name="up_projection",
        out_shape=(
            jax.ShapeDtypeStruct((count, width), BF16),
            jax.ShapeDtypeStruct((own, count), BF16),
            jax.ShapeDtypeStruct((rows, width), F32),
        ),
        in_specs=[pl.BlockSpec(memory_space=pltpu.HBM)] * 5,
        out_specs=(vmem, vmem, vmem),
        scratch_shapes=scratch,
        compiler_params=pltpu.CompilerParams(
            collective_id=0, has_side_effects=True, vmem_limit_bytes=VMEM
        ),
    )(tokens.T, weight_codes, weight_scales.T, cotangent, grad_exponents.T)
    return projected, token_grad.T, weight_grad


def solution(mesh):
    placed = P("node", "cross")
    return jax.shard_map(
        on_device,
        mesh=mesh,
        in_specs=(placed,) * 5,
        out_specs=(placed,) * 3,
        check_vma=False,
    )
```

```python
import jax
import jax.numpy as jnp
from jax import lax
from jax.experimental import pallas as pl
from jax.experimental.pallas import tpu as pltpu
from jax.sharding import PartitionSpec as P

QBLOCK = 128
VMEM = 58 << 20
NY, NZ, NX = 8, 4, 4
HERE = NY // 2
PARTS = 2
MESH = pl.DeviceIdType.MESH
F32, BF16 = jnp.float32, jnp.bfloat16


def kernel(
    tok_hbm, code_hbm, scale_hbm, cot_hbm, exp_hbm,
    out_ref, tgrad_ref, wgrad_ref,
    tok, code, scale, expo, wts, cot, feats, narrow, part, from_core, summed,
    from_x, reduced, from_z, final, home, prod, ring, wg_send, wg_recv,
    in_s, to_s, to_r, cot_s, cot_r, one_s, one_r, tz_s, tz_r, tx_s, tx_r, tk_s, tk_r,
    gk_s, gk_r, gx_s, gx_r, gz_s, gz_r, ring_s, ring_r,
):
    node, cross = lax.axis_index("node"), lax.axis_index("cross")
    y, zl = node // 2, node % 2
    zh, x, k = cross // 8, (cross // 2) % NX, cross % 2
    tokens, width = cot_hbm.shape
    half = tokens // 2
    rows = code_hbm.shape[0]
    own = tok_hbm.shape[0]

    own_slot = cot.at[HERE]
    loads = [
        pltpu.make_async_copy(src, dst, in_s.at[i])
        for i, (src, dst) in enumerate(
            [(tok_hbm, tok), (cot_hbm, own_slot), (code_hbm, code), (scale_hbm, scale), (exp_hbm, expo)]
        )
    ]
    for load in loads:
        load.start()

    def at(y=y, zl=zl, zh=zh, x=x, k=k):
        return (y * 2 + zl, zh * 8 + x * 2 + k)

    up, down = at(y=(y + 1) % NY), at(y=(y + NY - 1) % NY)
    pair = at(zl=1 - zl)
    core = at(k=1 - k)
    zs = [at(zh=(zh + o) % NZ) for o in range(1, NZ)]
    xs = [at(x=(x + o) % NX) for o in range(1, NX)]
    place = 2 * zh + x // 2
    slot_there = (y - place + HERE + NY) % NY
    owner = at(y=place, zh=slot_there // 2, x=2 * (slot_there % 2) + x % 2)
    home_of = at(y=(y + NY - HERE + place) % NY, zh=y // 2, x=2 * (y % 2) + x % 2)
    moves = jnp.logical_or(place != y, place != HERE)

    def remote(src, dst, send, recv, device):
        return pltpu.make_async_remote_copy(
            src_ref=src, dst_ref=dst, send_sem=send, recv_sem=recv,
            device_id=device, device_id_type=MESH,
        )

    def landed(slot, recv):
        remote(slot, slot, one_s.at[0], recv, core).wait_recv()

    started = []

    def go(copy):
        copy.start()
        started.append(copy)

    def columns(blocks):
        count = blocks.shape[0]
        narrow[...] = jnp.zeros_like(narrow)
        narrow[:count, :rows] = blocks
        return narrow[...].T[:rows, :count]

    barrier = pltpu.get_barrier_semaphore()
    friends = [up, down, pair, core] + zs + xs

    def greet(device):
        pl.semaphore_signal(barrier, inc=1, device_id=device, device_id_type=MESH)

    for device in friends:
        greet(device)

    @pl.when(moves)
    def _():
        greet(owner)
        greet(home_of)

    pl.semaphore_wait(barrier, len(friends) + 2 * moves.astype(jnp.int32))

    size = own // PARTS

    def spot(e, g, p=None):
        start = g * own if p is None else g * own + p * size
        return feats.at[e, pl.ds(pl.multiple_of(start, 16), own if p is None else size)]

    own_g = 2 * (x % 2) + k
    to_owner = [
        remote(tok.at[pl.ds(p * size, size)], spot(slot_there, own_g, p), to_s.at[p], to_r.at[p], owner)
        for p in range(PARTS)
    ]

    def tok_start():
        @pl.when(moves)
        def _():
            for copy in to_owner:
                copy.start()

        @pl.when(jnp.logical_not(moves))
        def _():
            spot(place, own_g)[...] = tok[...]

    def tok_send_x(j, p):
        src = spot(2 * j + x // 2, own_g, p)
        for o in (1, 3, 2):
            go(remote(src, src, tx_s.at[j, o - 1, p], tx_r.at[j, o - 1, p], xs[o - 1]))

    def tok_send_core(e, xl):
        src = spot(e, 2 * xl + k)
        go(remote(src, src, tk_s.at[e, xl], tk_r.at[e, xl], core))

    def tok_own():
        for p in range(PARTS):
            src = spot(place, own_g, p)

            @pl.when(moves)
            def _():
                landed(src, to_r.at[p])

            for o in range(1, NZ):
                go(remote(src, src, tz_s.at[o - 1, p], tz_r.at[zh, p], zs[o - 1]))
            tok_send_x(zh, p)
        tok_send_core(place, x % 2)

    need = [0, 3, 1, 2]
    ahead = (zh > 0).astype(jnp.int32) + (zh % 3 > 0).astype(jnp.int32) + (zh == 2).astype(jnp.int32)
    turn_of = [zh]
    for m in range(NZ - 1):
        later = (ahead <= m).astype(jnp.int32)
        turn_of.append(need[m] + later * (need[m + 1] - need[m]))

    def tok_from_z(m):
        j = turn_of[m]
        e = 2 * j + x // 2
        for p in range(PARTS):
            landed(spot(e, own_g, p), tz_r.at[j, p])
            tok_send_x(j, p)
        tok_send_core(e, x % 2)

    def tok_from_x(m):
        j = turn_of[m]
        for o in (1, 3, 2):
            there = (x + o) % NX
            e = 2 * j + there // 2
            for p in range(PARTS):
                landed(spot(e, 2 * (there % 2) + k, p), tx_r.at[j, NX - o - 1, p])
            tok_send_core(e, there % 2)

    def tok_from_core(e):
        for xl in range(2):
            landed(spot(e, 2 * xl + 1 - k), tk_r.at[e, xl])

    own_rows = pl.ds(pl.multiple_of(zl * rows, 32), rows)
    other_rows = pl.ds(pl.multiple_of((1 - zl) * rows, 32), rows)
    wsend = remote(wts.at[own_rows], wts.at[own_rows], one_s.at[1], one_r.at[1], pair)

    def weights_own():
        loads[2].wait()
        loads[3].wait()
        scales = columns(scale[...])
        for b in range(width // QBLOCK):
            cols = slice(b * QBLOCK, (b + 1) * QBLOCK)
            wts[own_rows, cols] = (
                code[:, cols].astype(F32) * scales[:, b : b + 1]
            ).astype(BF16)

    def weights_send():
        go(wsend)

    def weights_other():
        landed(wts.at[other_rows], one_r.at[1])

    hs = [pl.ds(0, half), pl.ds(half, half)]
    ways = [(up, -1), (down, 1)]

    def cot_slot(way, s):
        return (HERE + ways[way][1] * s + NY) % NY

    def cot_copy(way, h, s):
        return remote(
            cot.at[cot_slot(way, s), hs[h]], cot.at[cot_slot(way, s + 1), hs[h]],
            cot_s.at[way, h, s], cot_r.at[way, h, s], ways[way][0],
        )

    def cot_start():
        for i in range(2):
            for way in range(2):
                go(cot_copy(way, (i + way) % 2, 0))

    def cot_step(i):
        s = i // 2
        for way in range(2):
            h = (i + way) % 2
            landed(cot.at[cot_slot(way, s + 1), hs[h]], cot_r.at[way, h, s])
            if i < 5:
                go(cot_copy(way, h, s + 1))

    def tg_part(i):
        e = (HERE + i) % NY
        part[e] = lax.dot_general(
            wts[...], cot[e], (((1,), (1,)), ((), ())), preferred_element_type=F32
        ).astype(BF16)
        for xl in range(2):
            src = part.at[e, pl.ds(pl.multiple_of((2 * xl + 1 - k) * own, 32), own)]
            go(remote(src, from_core.at[e, xl], gk_s.at[e, xl], gk_r.at[e, xl], core))

    def tg_x_copy(e, xl):
        there = 2 * (e % 2) + xl
        o = (x - there + NX) % NX
        slot = lax.max(o - 1, 0)
        return there != x, remote(
            summed.at[e, xl], from_x.at[e // 2, slot], gx_s.at[e, xl],
            gx_r.at[e // 2, slot], at(x=there),
        )

    def tg_sum(i):
        e = (HERE + i) % NY
        for xl in range(2):
            slot = from_core.at[e, xl]
            landed(slot, gk_r.at[e, xl])
            mine = part[e, pl.ds(pl.multiple_of((2 * xl + k) * own, 32), own)]
            summed[e, xl] = (mine.astype(F32) + slot[...].astype(F32)).astype(BF16)
            leaves, copy = tg_x_copy(e, xl)

            @pl.when(leaves)
            def _():
                copy.start()

    def tg_z_copy(j):
        o = (zh - j + NZ) % NZ
        slot = lax.max(o - 1, 0)
        return j != zh, remote(
            reduced.at[j], from_z.at[slot], gz_s.at[j], gz_r.at[slot], at(zh=j)
        )

    def tg_from_x(j):
        total = summed[2 * j + x // 2, x % 2].astype(F32)
        for o in range(NX - 1):
            landed(from_x.at[j, o], gx_r.at[j, o])
            total += from_x[j, o].astype(F32)
        reduced[j] = total.astype(BF16)
        leaves, copy = tg_z_copy(j)

        @pl.when(leaves)
        def _():
            copy.start()

    to_home = remote(final, home, one_s.at[2], one_r.at[2], home_of)

    def tg_from_z():
        total = reduced[zh].astype(F32)
        for o in range(NZ - 1):
            landed(from_z.at[o], gz_r.at[o])
            total += from_z[o].astype(F32)
        final[...] = total.astype(BF16)

        @pl.when(moves)
        def _():
            to_home.start()

    def tg_end():
        @pl.when(moves)
        def _():
            to_home.wait_recv()
            tgrad_ref[...] = home[...]

        @pl.when(jnp.logical_not(moves))
        def _():
            tgrad_ref[...] = final[...]

    def product(i):
        e = (HERE + i) % NY
        prod[e] = lax.dot_general(
            feats[e], wts[...], (((0,), (0,)), ((), ())), preferred_element_type=F32
        )

    def ring_copy(way, i):
        return remote(
            ring.at[way, i], ring.at[way, i + 2], ring_s.at[way, i], ring_r.at[way, i], ways[way][0]
        )

    def ring_goal(way, i):
        steps = (4 if i % 2 == 0 else 3) - i // 2
        return (HERE - ways[way][1] * steps + NY) % NY

    def ring_start(way, i):
        h = (i + way) % 2
        ring[way, i] = prod[ring_goal(way, i), hs[h]].astype(BF16)
        go(ring_copy(way, i))

    def ring_step(i):
        for way in range(2):
            h = (i + way) % 2
            slot = ring.at[way, i + 2]
            landed(slot, ring_r.at[way, i])
            if i < 5:
                slot[...] = (
                    slot[...].astype(F32) + prod[ring_goal(way, i + 2), hs[h]]
                ).astype(BF16)
                go(ring_copy(way, i + 2))

    def wg_half(which):
        total = jnp.zeros((rows, width), F32)
        for e in range(NY):
            total += jnp.dot(feats[e, which], cot[e], preferred_element_type=F32)
        return total

    wg_copy = remote(wg_send, wg_recv, one_s.at[3], one_r.at[3], pair)

    def wg_start():
        wg_send[...] = wg_half(other_rows).astype(BF16)
        go(wg_copy)

    def wg_own():
        wgrad_ref[...] = wg_half(own_rows)

    def wg_end():
        wg_copy.wait_recv()
        factor = columns(jnp.exp2(-expo[...].astype(F32)))
        for b in range(width // QBLOCK):
            cols = slice(b * QBLOCK, (b + 1) * QBLOCK)
            wgrad_ref[:, cols] = (
                wgrad_ref[:, cols] + wg_recv[:, cols].astype(F32)
            ) * factor[:, b : b + 1]

    loads[0].wait()
    tok_start()
    loads[1].wait()
    cot_start()
    weights_own()
    weights_send()
    loads[4].wait()
    cot_step(0)
    tok_own()
    cot_step(1)
    tok_from_z(1)
    cot_step(2)
    tok_from_z(2)
    weights_other()
    tg_part(0)
    tok_from_x(0)
    tg_part(1)
    tg_part(-1)
    cot_step(3)
    tok_from_x(1)
    tok_from_z(3)
    tg_sum(0)
    tg_sum(1)
    tg_sum(-1)
    cot_step(4)
    tok_from_x(2)
    tok_from_core(0)
    tok_from_core(1)
    tok_from_core(7)
    product(4)
    ring_start(0, 0)
    ring_start(1, 0)
    product(3)
    ring_start(0, 1)
    product(-3)
    ring_start(1, 1)
    tg_part(2)
    tg_part(-2)
    tg_sum(2)
    tg_sum(-2)
    cot_step(5)
    tg_part(3)
    tg_part(-3)
    tok_from_x(3)
    tg_sum(3)
    tg_sum(-3)
    cot_step(6)
    tg_part(4)
    tok_from_core(6)
    tok_from_core(2)
    tg_sum(4)
    product(2)
    product(-2)
    ring_step(0)
    tg_from_x(2)
    tok_from_core(5)
    tok_from_core(3)
    tok_from_core(4)
    wg_start()
    ring_step(1)
    tg_from_x(1)
    tg_from_x(3)
    product(1)
    product(-1)
    ring_step(2)
    product(0)
    ring_step(3)
    tg_from_x(0)
    ring_step(4)
    tg_from_z()
    wg_own()
    wg_end()
    ring_step(5)
    tg_end()
    ring_step(6)
    for h in range(2):
        out_ref[hs[h]] = (
            prod[HERE, hs[h]]
            + ring[0, 8 - h].astype(F32)
            + ring[1, 7 + h].astype(F32)
        ).astype(BF16)

    for copy in started:
        copy.wait_send()
    some = [tg_x_copy(e, xl) for e in range(NY) for xl in range(2)]
    some += [tg_z_copy(j) for j in range(NZ)]
    some += [(moves, copy) for copy in to_owner + [to_home]]
    for leaves, copy in some:

        @pl.when(leaves)
        def _():
            copy.wait_send()


def on_device(tokens, weight_codes, weight_scales, cotangent, grad_exponents):
    count, own = tokens.shape
    rows, width = weight_codes.shape
    depth = 2 * rows
    dma = pltpu.SemaphoreType.DMA
    vmem = pl.BlockSpec(memory_space=pltpu.VMEM)
    scratch = [
        pltpu.VMEM((own, count), BF16),
        pltpu.VMEM((rows, width), jnp.int32),
        pltpu.VMEM((width // QBLOCK, rows), F32),
        pltpu.VMEM((width // QBLOCK, rows), jnp.int32),
        pltpu.VMEM((depth, width), BF16),
        pltpu.VMEM((NY, count, width), BF16),
        pltpu.VMEM((NY, depth, count), BF16),
        pltpu.VMEM((8, -(-rows // 128) * 128), F32),
        pltpu.VMEM((NY, depth, count), BF16),
        pltpu.VMEM((NY, 2, own, count), BF16),
        pltpu.VMEM((NY, 2, own, count), BF16),
        pltpu.VMEM((NZ, NX - 1, own, count), BF16),
        pltpu.VMEM((NZ, own, count), BF16),
        pltpu.VMEM((NZ - 1, own, count), BF16),
        pltpu.VMEM((own, count), BF16),
        pltpu.VMEM((own, count), BF16),
        pltpu.VMEM((NY, count, width), F32),
        pltpu.VMEM((2, 9, count // 2, width), BF16),
        pltpu.VMEM((rows, width), BF16),
        pltpu.VMEM((rows, width), BF16),
        dma((5,)),
        dma((PARTS,)), dma((PARTS,)),
        dma((2, 2, 4)), dma((2, 2, 4)),
        dma((4,)), dma((4,)),
        dma((NZ - 1, PARTS)), dma((NZ, PARTS)),
        dma((NZ, NX - 1, PARTS)), dma((NZ, NX - 1, PARTS)),
        dma((NY, 2)), dma((NY, 2)),
        dma((NY, 2)), dma((NY, 2)),
        dma((NY, 2)), dma((NZ, NX - 1)),
        dma((NZ,)), dma((NZ - 1,)),
        dma((2, 7)), dma((2, 7)),
    ]
    projected, token_grad, weight_grad = pl.pallas_call(
        kernel,
        name="up_projection",
        out_shape=(
            jax.ShapeDtypeStruct((count, width), BF16),
            jax.ShapeDtypeStruct((own, count), BF16),
            jax.ShapeDtypeStruct((rows, width), F32),
        ),
        in_specs=[pl.BlockSpec(memory_space=pltpu.HBM)] * 5,
        out_specs=(vmem, vmem, vmem),
        scratch_shapes=scratch,
        compiler_params=pltpu.CompilerParams(
            collective_id=0, has_side_effects=True, vmem_limit_bytes=VMEM
        ),
    )(tokens.T, weight_codes, weight_scales.T, cotangent, grad_exponents.T)
    return projected, token_grad.T, weight_grad


def solution(mesh):
    placed = P("node", "cross")
    return jax.shard_map(
        on_device,
        mesh=mesh,
        in_specs=(placed,) * 5,
        out_specs=(placed,) * 3,
        check_vma=False,
    )
```

```python
import jax
import jax.numpy as jnp
from jax import lax
from jax.experimental import pallas as pl
from jax.experimental.pallas import tpu as pltpu
from jax.sharding import PartitionSpec as P

QBLOCK = 128
VMEM = 58 << 20
NY, NZ, NX = 8, 4, 4
HERE = NY // 2
PARTS = 2
MESH = pl.DeviceIdType.MESH
F32, BF16 = jnp.float32, jnp.bfloat16


def kernel(
    tok_hbm, code_hbm, scale_hbm, cot_hbm, exp_hbm,
    out_ref, tgrad_ref, wgrad_ref,
    tok, code, scale, expo, held, wts, cot, feats, narrow, part, from_core, summed,
    from_x, reduced, from_z, final, back, home, prod, ring, wg_send, wg_recv,
    in_s, ta_s, ta_r, to_s, to_r, cot_s, cot_r, one_s, one_r, tz_s, tz_r, tx_s, tx_r, tk_s, tk_r,
    gk_s, gk_r, gx_s, gx_r, gz_s, gz_r, ring_s, ring_r,
):
    node, cross = lax.axis_index("node"), lax.axis_index("cross")
    y, zl = node // 2, node % 2
    zh, x, k = cross // 8, (cross // 2) % NX, cross % 2
    tokens, width = cot_hbm.shape
    half = tokens // 2
    rows = code_hbm.shape[0]
    own = tok_hbm.shape[0]

    own_slot = cot.at[HERE]
    loads = [
        pltpu.make_async_copy(src, dst, in_s.at[i])
        for i, (src, dst) in enumerate(
            [(tok_hbm, tok), (cot_hbm, own_slot), (code_hbm, code), (scale_hbm, scale), (exp_hbm, expo)]
        )
    ]
    for load in loads:
        load.start()

    def at(y=y, zl=zl, zh=zh, x=x, k=k):
        return (y * 2 + zl, zh * 8 + x * 2 + k)

    up, down = at(y=(y + 1) % NY), at(y=(y + NY - 1) % NY)
    pair = at(zl=1 - zl)
    core = at(k=1 - k)
    zs = [at(zh=(zh + o) % NZ) for o in range(1, NZ)]
    xs = [at(x=(x + o) % NX) for o in range(1, NX)]
    place = 2 * zh + x // 2
    goal = (y - place + HERE + NY) % NY
    turn = at(zh=goal // 2, x=2 * (goal % 2) + x % 2)
    turns = goal != place
    fore = at(y=(y + NY + HERE - place) % NY)
    aft = at(y=(y + NY - HERE + place) % NY)
    shifts = place != HERE

    def remote(src, dst, send, recv, device):
        return pltpu.make_async_remote_copy(
            src_ref=src, dst_ref=dst, send_sem=send, recv_sem=recv,
            device_id=device, device_id_type=MESH,
        )

    def landed(slot, recv):
        remote(slot, slot, one_s.at[0], recv, core).wait_recv()

    started = []

    def go(copy):
        copy.start()
        started.append(copy)

    def columns(blocks):
        count = blocks.shape[0]
        narrow[...] = jnp.zeros_like(narrow)
        narrow[:count, :rows] = blocks
        return narrow[...].T[:rows, :count]

    barrier = pltpu.get_barrier_semaphore()
    friends = [up, down, pair, core] + zs + xs

    def greet(device):
        pl.semaphore_signal(barrier, inc=1, device_id=device, device_id_type=MESH)

    for device in friends:
        greet(device)

    @pl.when(turns)
    def _():
        greet(turn)

    @pl.when(shifts)
    def _():
        greet(fore)
        greet(aft)

    pl.semaphore_wait(
        barrier, len(friends) + turns.astype(jnp.int32) + 2 * shifts.astype(jnp.int32)
    )

    size = own // PARTS

    def spot(e, g, p=None):
        start = g * own if p is None else g * own + p * size
        return feats.at[e, pl.ds(pl.multiple_of(start, 16), own if p is None else size)]

    own_g = 2 * (x % 2) + k
    bits = [pl.ds(p * size, size) for p in range(PARTS)]
    to_turn = [
        remote(tok.at[bits[p]], held.at[bits[p]], ta_s.at[p], ta_r.at[p], turn)
        for p in range(PARTS)
    ]
    to_fore = [
        remote(held.at[bits[p]], spot(place, own_g, p), to_s.at[p], to_r.at[p], fore)
        for p in range(PARTS)
    ]

    def tok_start():
        @pl.when(turns)
        def _():
            for copy in to_turn:
                copy.start()

        @pl.when(jnp.logical_not(turns))
        def _():
            held[...] = tok[...]

    def tok_shift():
        for p in range(PARTS):
            @pl.when(turns)
            def _():
                landed(held.at[bits[p]], ta_r.at[p])

            @pl.when(shifts)
            def _():
                to_fore[p].start()

            @pl.when(jnp.logical_not(shifts))
            def _():
                spot(place, own_g, p)[...] = held[bits[p]]

    def tok_send_x(j, p):
        src = spot(2 * j + x // 2, own_g, p)
        for o in (1, 3, 2):
            go(remote(src, src, tx_s.at[j, o - 1, p], tx_r.at[j, o - 1, p], xs[o - 1]))

    def tok_send_core(e, xl):
        src = spot(e, 2 * xl + k)
        go(remote(src, src, tk_s.at[e, xl], tk_r.at[e, xl], core))

    def tok_own():
        for p in range(PARTS):
            src = spot(place, own_g, p)

            @pl.when(shifts)
            def _():
                landed(src, to_r.at[p])

            for o in range(1, NZ):
                go(remote(src, src, tz_s.at[o - 1, p], tz_r.at[zh, p], zs[o - 1]))
            tok_send_x(zh, p)
        tok_send_core(place, x % 2)

    need = [0, 3, 1, 2]
    ahead = (zh > 0).astype(jnp.int32) + (zh % 3 > 0).astype(jnp.int32) + (zh == 2).astype(jnp.int32)
    turn_of = [zh]
    for m in range(NZ - 1):
        later = (ahead <= m).astype(jnp.int32)
        turn_of.append(need[m] + later * (need[m + 1] - need[m]))

    def tok_from_z(m):
        j = turn_of[m]
        e = 2 * j + x // 2
        for p in range(PARTS):
            landed(spot(e, own_g, p), tz_r.at[j, p])
            tok_send_x(j, p)
        tok_send_core(e, x % 2)

    def tok_from_x(m):
        j = turn_of[m]
        for o in (1, 3, 2):
            there = (x + o) % NX
            e = 2 * j + there // 2
            for p in range(PARTS):
                landed(spot(e, 2 * (there % 2) + k, p), tx_r.at[j, NX - o - 1, p])
            tok_send_core(e, there % 2)

    def tok_from_core(e):
        for xl in range(2):
            landed(spot(e, 2 * xl + 1 - k), tk_r.at[e, xl])

    own_rows = pl.ds(pl.multiple_of(zl * rows, 32), rows)
    other_rows = pl.ds(pl.multiple_of((1 - zl) * rows, 32), rows)
    wsend = remote(wts.at[own_rows], wts.at[own_rows], one_s.at[1], one_r.at[1], pair)

    def weights_own():
        loads[2].wait()
        loads[3].wait()
        scales = columns(scale[...])
        for b in range(width // QBLOCK):
            cols = slice(b * QBLOCK, (b + 1) * QBLOCK)
            wts[own_rows, cols] = (
                code[:, cols].astype(F32) * scales[:, b : b + 1]
            ).astype(BF16)

    def weights_send():
        go(wsend)

    def weights_other():
        landed(wts.at[other_rows], one_r.at[1])

    hs = [pl.ds(0, half), pl.ds(half, half)]
    ways = [(up, -1), (down, 1)]

    def cot_slot(way, s):
        return (HERE + ways[way][1] * s + NY) % NY

    def cot_copy(way, h, s):
        return remote(
            cot.at[cot_slot(way, s), hs[h]], cot.at[cot_slot(way, s + 1), hs[h]],
            cot_s.at[way, h, s], cot_r.at[way, h, s], ways[way][0],
        )

    def cot_start():
        for i in range(2):
            for way in range(2):
                go(cot_copy(way, (i + way) % 2, 0))

    def cot_step(i):
        s = i // 2
        for way in range(2):
            h = (i + way) % 2
            landed(cot.at[cot_slot(way, s + 1), hs[h]], cot_r.at[way, h, s])
            if i < 5:
                go(cot_copy(way, h, s + 1))

    def tg_part(i):
        e = (HERE + i) % NY
        part[e] = lax.dot_general(
            wts[...], cot[e], (((1,), (1,)), ((), ())), preferred_element_type=F32
        ).astype(BF16)
        for xl in range(2):
            src = part.at[e, pl.ds(pl.multiple_of((2 * xl + 1 - k) * own, 32), own)]
            go(remote(src, from_core.at[e, xl], gk_s.at[e, xl], gk_r.at[e, xl], core))

    def tg_x_copy(e, xl):
        there = 2 * (e % 2) + xl
        o = (x - there + NX) % NX
        slot = lax.max(o - 1, 0)
        return there != x, remote(
            summed.at[e, xl], from_x.at[e // 2, slot], gx_s.at[e, xl],
            gx_r.at[e // 2, slot], at(x=there),
        )

    def tg_sum(i):
        e = (HERE + i) % NY
        for xl in range(2):
            slot = from_core.at[e, xl]
            landed(slot, gk_r.at[e, xl])
            mine = part[e, pl.ds(pl.multiple_of((2 * xl + k) * own, 32), own)]
            summed[e, xl] = (mine.astype(F32) + slot[...].astype(F32)).astype(BF16)
            leaves, copy = tg_x_copy(e, xl)

            @pl.when(leaves)
            def _():
                copy.start()

    def tg_z_copy(j):
        o = (zh - j + NZ) % NZ
        slot = lax.max(o - 1, 0)
        return j != zh, remote(
            reduced.at[j], from_z.at[slot], gz_s.at[j], gz_r.at[slot], at(zh=j)
        )

    def tg_from_x(j):
        total = summed[2 * j + x // 2, x % 2].astype(F32)
        for o in range(NX - 1):
            landed(from_x.at[j, o], gx_r.at[j, o])
            total += from_x[j, o].astype(F32)
        reduced[j] = total.astype(BF16)
        leaves, copy = tg_z_copy(j)

        @pl.when(leaves)
        def _():
            copy.start()

    to_aft = remote(final, back, one_s.at[2], one_r.at[2], aft)
    to_home = remote(back, home, one_s.at[0], one_r.at[0], turn)

    def tg_from_z():
        total = reduced[zh].astype(F32)
        for o in range(NZ - 1):
            landed(from_z.at[o], gz_r.at[o])
            total += from_z[o].astype(F32)
        final[...] = total.astype(BF16)

        @pl.when(shifts)
        def _():
            to_aft.start()

    def tg_turn():
        @pl.when(shifts)
        def _():
            to_aft.wait_recv()

        @pl.when(jnp.logical_not(shifts))
        def _():
            back[...] = final[...]

        @pl.when(turns)
        def _():
            to_home.start()

    def tg_end():
        @pl.when(turns)
        def _():
            to_home.wait_recv()
            tgrad_ref[...] = home[...]

        @pl.when(jnp.logical_not(turns))
        def _():
            tgrad_ref[...] = back[...]

    def product(i):
        e = (HERE + i) % NY
        prod[e] = lax.dot_general(
            feats[e], wts[...], (((0,), (0,)), ((), ())), preferred_element_type=F32
        )

    def ring_copy(way, i):
        return remote(
            ring.at[way, i], ring.at[way, i + 2], ring_s.at[way, i], ring_r.at[way, i], ways[way][0]
        )

    def ring_goal(way, i):
        steps = (4 if i % 2 == 0 else 3) - i // 2
        return (HERE - ways[way][1] * steps + NY) % NY

    def ring_start(way, i):
        h = (i + way) % 2
        ring[way, i] = prod[ring_goal(way, i), hs[h]].astype(BF16)
        go(ring_copy(way, i))

    def ring_step(i):
        for way in range(2):
            h = (i + way) % 2
            slot = ring.at[way, i + 2]
            landed(slot, ring_r.at[way, i])
            if i < 5:
                slot[...] = (
                    slot[...].astype(F32) + prod[ring_goal(way, i + 2), hs[h]]
                ).astype(BF16)
                go(ring_copy(way, i + 2))

    def wg_half(which):
        total = jnp.zeros((rows, width), F32)
        for e in range(NY):
            total += jnp.dot(feats[e, which], cot[e], preferred_element_type=F32)
        return total

    wg_copy = remote(wg_send, wg_recv, one_s.at[3], one_r.at[3], pair)

    def wg_start():
        wg_send[...] = wg_half(other_rows).astype(BF16)
        go(wg_copy)

    def wg_own():
        wgrad_ref[...] = wg_half(own_rows)

    def wg_end():
        wg_copy.wait_recv()
        factor = columns(jnp.exp2(-expo[...].astype(F32)))
        for b in range(width // QBLOCK):
            cols = slice(b * QBLOCK, (b + 1) * QBLOCK)
            wgrad_ref[:, cols] = (
                wgrad_ref[:, cols] + wg_recv[:, cols].astype(F32)
            ) * factor[:, b : b + 1]

    loads[0].wait()
    tok_start()
    loads[1].wait()
    cot_start()
    weights_own()
    weights_send()
    loads[4].wait()
    tok_shift()
    cot_step(0)
    tok_own()
    cot_step(1)
    tok_from_z(1)
    cot_step(2)
    tok_from_z(2)
    weights_other()
    tg_part(0)
    tok_from_x(0)
    tg_part(1)
    tg_part(-1)
    cot_step(3)
    tok_from_x(1)
    tok_from_z(3)
    cot_step(4)
    tok_from_core(0)
    tok_from_core(1)
    product(4)
    ring_start(0, 0)
    ring_start(1, 0)
    product(-3)
    ring_start(1, 1)
    tg_sum(0)
    tg_sum(1)
    tg_sum(-1)
    tok_from_x(2)
    tok_from_core(7)
    product(3)
    ring_start(0, 1)
    tg_part(2)
    tg_part(-2)
    tg_sum(2)
    tg_sum(-2)
    cot_step(5)
    tg_part(3)
    tg_part(-3)
    tok_from_x(3)
    tg_sum(3)
    tg_sum(-3)
    cot_step(6)
    tg_part(4)
    tok_from_core(6)
    tok_from_core(2)
    tg_sum(4)
    product(2)
    product(-2)
    ring_step(0)
    tg_from_x(2)
    tok_from_core(5)
    tok_from_core(3)
    tok_from_core(4)
    wg_start()
    ring_step(1)
    tg_from_x(1)
    tg_from_x(3)
    product(1)
    product(-1)
    ring_step(2)
    product(0)
    tg_from_x(0)
    ring_step(3)
    ring_step(4)
    tg_from_z()
    wg_own()
    tg_turn()
    wg_end()
    ring_step(5)
    ring_step(6)
    for h in range(2):
        out_ref[hs[h]] = (
            prod[HERE, hs[h]]
            + ring[0, 8 - h].astype(F32)
            + ring[1, 7 + h].astype(F32)
        ).astype(BF16)

    tg_end()

    for copy in started:
        copy.wait_send()
    some = [tg_x_copy(e, xl) for e in range(NY) for xl in range(2)]
    some += [tg_z_copy(j) for j in range(NZ)]
    some += [(turns, copy) for copy in to_turn + [to_home]]
    some += [(shifts, copy) for copy in to_fore + [to_aft]]
    for leaves, copy in some:

        @pl.when(leaves)
        def _():
            copy.wait_send()


def on_device(tokens, weight_codes, weight_scales, cotangent, grad_exponents):
    count, own = tokens.shape
    rows, width = weight_codes.shape
    depth = 2 * rows
    dma = pltpu.SemaphoreType.DMA
    vmem = pl.BlockSpec(memory_space=pltpu.VMEM)
    scratch = [
        pltpu.VMEM((own, count), BF16),
        pltpu.VMEM((rows, width), jnp.int32),
        pltpu.VMEM((width // QBLOCK, rows), F32),
        pltpu.VMEM((width // QBLOCK, rows), jnp.int32),
        pltpu.VMEM((own, count), BF16),
        pltpu.VMEM((depth, width), BF16),
        pltpu.VMEM((NY, count, width), BF16),
        pltpu.VMEM((NY, depth, count), BF16),
        pltpu.VMEM((8, -(-rows // 128) * 128), F32),
        pltpu.VMEM((NY, depth, count), BF16),
        pltpu.VMEM((NY, 2, own, count), BF16),
        pltpu.VMEM((NY, 2, own, count), BF16),
        pltpu.VMEM((NZ, NX - 1, own, count), BF16),
        pltpu.VMEM((NZ, own, count), BF16),
        pltpu.VMEM((NZ - 1, own, count), BF16),
        pltpu.VMEM((own, count), BF16),
        pltpu.VMEM((own, count), BF16),
        pltpu.VMEM((own, count), BF16),
        pltpu.VMEM((NY, count, width), F32),
        pltpu.VMEM((2, 9, count // 2, width), BF16),
        pltpu.VMEM((rows, width), BF16),
        pltpu.VMEM((rows, width), BF16),
        dma((5,)),
        dma((PARTS,)), dma((PARTS,)),
        dma((PARTS,)), dma((PARTS,)),
        dma((2, 2, 4)), dma((2, 2, 4)),
        dma((4,)), dma((4,)),
        dma((NZ - 1, PARTS)), dma((NZ, PARTS)),
        dma((NZ, NX - 1, PARTS)), dma((NZ, NX - 1, PARTS)),
        dma((NY, 2)), dma((NY, 2)),
        dma((NY, 2)), dma((NY, 2)),
        dma((NY, 2)), dma((NZ, NX - 1)),
        dma((NZ,)), dma((NZ - 1,)),
        dma((2, 7)), dma((2, 7)),
    ]
    projected, token_grad, weight_grad = pl.pallas_call(
        kernel,
        name="up_projection",
        out_shape=(
            jax.ShapeDtypeStruct((count, width), BF16),
            jax.ShapeDtypeStruct((own, count), BF16),
            jax.ShapeDtypeStruct((rows, width), F32),
        ),
        in_specs=[pl.BlockSpec(memory_space=pltpu.HBM)] * 5,
        out_specs=(vmem, vmem, vmem),
        scratch_shapes=scratch,
        compiler_params=pltpu.CompilerParams(
            collective_id=0, has_side_effects=True, vmem_limit_bytes=VMEM
        ),
    )(tokens.T, weight_codes, weight_scales.T, cotangent, grad_exponents.T)
    return projected, token_grad.T, weight_grad


def solution(mesh):
    placed = P("node", "cross")
    return jax.shard_map(
        on_device,
        mesh=mesh,
        in_specs=(placed,) * 5,
        out_specs=(placed,) * 3,
        check_vma=False,
    )
```

```python
import jax
import jax.numpy as jnp
from jax import lax
from jax.experimental import pallas as pl
from jax.experimental.pallas import tpu as pltpu
from jax.sharding import PartitionSpec as P

QBLOCK = 128
VMEM = 58 << 20
NY, NZ, NX = 8, 4, 4
HERE = NY // 2
PARTS = 2
MESH = pl.DeviceIdType.MESH
F32, BF16 = jnp.float32, jnp.bfloat16


def kernel(
    tok_hbm, code_hbm, scale_hbm, cot_hbm, exp_hbm,
    out_ref, tgrad_ref, wgrad_ref,
    tok, code, scale, expo, held, wts, cot, feats, narrow, part, from_core, summed,
    from_x, reduced, from_z, final, back, home, prod, ring, wg_send, wg_recv,
    in_s, ta_s, ta_r, to_s, to_r, cot_s, cot_r, one_s, one_r, tz_s, tz_r, tx_s, tx_r, tk_s, tk_r,
    gk_s, gk_r, gx_s, gx_r, gz_s, gz_r, ring_s, ring_r,
):
    node, cross = lax.axis_index("node"), lax.axis_index("cross")
    y, zl = node // 2, node % 2
    zh, x, k = cross // 8, (cross // 2) % NX, cross % 2
    tokens, width = cot_hbm.shape
    half = tokens // 2
    rows = code_hbm.shape[0]
    own = tok_hbm.shape[0]

    own_slot = cot.at[HERE]
    loads = [
        pltpu.make_async_copy(src, dst, in_s.at[i])
        for i, (src, dst) in enumerate(
            [(tok_hbm, tok), (cot_hbm, own_slot), (code_hbm, code), (scale_hbm, scale), (exp_hbm, expo)]
        )
    ]
    for load in loads:
        load.start()

    def at(y=y, zl=zl, zh=zh, x=x, k=k):
        return (y * 2 + zl, zh * 8 + x * 2 + k)

    up, down = at(y=(y + 1) % NY), at(y=(y + NY - 1) % NY)
    pair = at(zl=1 - zl)
    core = at(k=1 - k)
    zs = [at(zh=(zh + o) % NZ) for o in range(1, NZ)]
    xs = [at(x=(x + o) % NX) for o in range(1, NX)]
    place = 2 * zh + x // 2
    goal = (y - place + HERE + NY) % NY
    turn = at(zh=goal // 2, x=2 * (goal % 2) + x % 2)
    turns = goal != place
    fore = at(y=(y + NY + HERE - place) % NY)
    aft = at(y=(y + NY - HERE + place) % NY)
    shifts = place != HERE

    def remote(src, dst, send, recv, device):
        return pltpu.make_async_remote_copy(
            src_ref=src, dst_ref=dst, send_sem=send, recv_sem=recv,
            device_id=device, device_id_type=MESH,
        )

    def landed(slot, recv):
        remote(slot, slot, one_s.at[0], recv, core).wait_recv()

    started = []

    def go(copy):
        copy.start()
        started.append(copy)

    def columns(blocks):
        count = blocks.shape[0]
        narrow[...] = jnp.zeros_like(narrow)
        narrow[:count, :rows] = blocks
        return narrow[...].T[:rows, :count]

    barrier = pltpu.get_barrier_semaphore()
    friends = [up, down, pair, core] + zs + xs

    def greet(device):
        pl.semaphore_signal(barrier, inc=1, device_id=device, device_id_type=MESH)

    for device in friends:
        greet(device)

    @pl.when(turns)
    def _():
        greet(turn)

    @pl.when(shifts)
    def _():
        greet(fore)
        greet(aft)

    pl.semaphore_wait(
        barrier, len(friends) + turns.astype(jnp.int32) + 2 * shifts.astype(jnp.int32)
    )

    size = own // PARTS

    def spot(e, g, p=None):
        start = g * own if p is None else g * own + p * size
        return feats.at[e, pl.ds(pl.multiple_of(start, 16), own if p is None else size)]

    own_g = 2 * (x % 2) + k
    bits = [pl.ds(p * size, size) for p in range(PARTS)]
    to_turn = [
        remote(tok.at[bits[p]], held.at[bits[p]], ta_s.at[p], ta_r.at[p], turn)
        for p in range(PARTS)
    ]
    to_fore = [
        remote(held.at[bits[p]], spot(place, own_g, p), to_s.at[p], to_r.at[p], fore)
        for p in range(PARTS)
    ]

    def tok_start():
        @pl.when(turns)
        def _():
            for copy in to_turn:
                copy.start()

        @pl.when(jnp.logical_not(turns))
        def _():
            held[...] = tok[...]

    def tok_shift():
        for p in range(PARTS):
            @pl.when(turns)
            def _():
                landed(held.at[bits[p]], ta_r.at[p])

            @pl.when(shifts)
            def _():
                to_fore[p].start()

            @pl.when(jnp.logical_not(shifts))
            def _():
                spot(place, own_g, p)[...] = held[bits[p]]

    def tok_send_x(j, p):
        src = spot(2 * j + x // 2, own_g, p)
        for o in (1, 3, 2):
            go(remote(src, src, tx_s.at[j, o - 1, p], tx_r.at[j, o - 1, p], xs[o - 1]))

    def tok_send_core(e, xl):
        src = spot(e, 2 * xl + k)
        go(remote(src, src, tk_s.at[e, xl], tk_r.at[e, xl], core))

    def tok_own():
        for p in range(PARTS):
            src = spot(place, own_g, p)

            @pl.when(shifts)
            def _():
                landed(src, to_r.at[p])

            for o in range(1, NZ):
                go(remote(src, src, tz_s.at[o - 1, p], tz_r.at[zh, p], zs[o - 1]))
            tok_send_x(zh, p)
        tok_send_core(place, x % 2)

    need = [0, 3, 1, 2]
    ahead = (zh > 0).astype(jnp.int32) + (zh % 3 > 0).astype(jnp.int32) + (zh == 2).astype(jnp.int32)
    turn_of = [zh]
    for m in range(NZ - 1):
        later = (ahead <= m).astype(jnp.int32)
        turn_of.append(need[m] + later * (need[m + 1] - need[m]))

    def tok_from_z(m):
        j = turn_of[m]
        e = 2 * j + x // 2
        for p in range(PARTS):
            landed(spot(e, own_g, p), tz_r.at[j, p])
            tok_send_x(j, p)
        tok_send_core(e, x % 2)

    def tok_from_x(m):
        j = turn_of[m]
        for o in (1, 3, 2):
            there = (x + o) % NX
            e = 2 * j + there // 2
            for p in range(PARTS):
                landed(spot(e, 2 * (there % 2) + k, p), tx_r.at[j, NX - o - 1, p])
            tok_send_core(e, there % 2)

    def tok_from_core(e):
        for xl in range(2):
            landed(spot(e, 2 * xl + 1 - k), tk_r.at[e, xl])

    own_rows = pl.ds(pl.multiple_of(zl * rows, 32), rows)
    other_rows = pl.ds(pl.multiple_of((1 - zl) * rows, 32), rows)
    wsend = remote(wts.at[own_rows], wts.at[own_rows], one_s.at[1], one_r.at[1], pair)

    def weights_own():
        loads[2].wait()
        loads[3].wait()
        scales = columns(scale[...])
        for b in range(width // QBLOCK):
            cols = slice(b * QBLOCK, (b + 1) * QBLOCK)
            wts[own_rows, cols] = (
                code[:, cols].astype(F32) * scales[:, b : b + 1]
            ).astype(BF16)

    def weights_send():
        go(wsend)

    def weights_other():
        landed(wts.at[other_rows], one_r.at[1])

    hs = [pl.ds(0, half), pl.ds(half, half)]
    ways = [(up, -1), (down, 1)]

    def cot_slot(way, s):
        return (HERE + ways[way][1] * s + NY) % NY

    def cot_copy(way, h, s):
        return remote(
            cot.at[cot_slot(way, s), hs[h]], cot.at[cot_slot(way, s + 1), hs[h]],
            cot_s.at[way, h, s], cot_r.at[way, h, s], ways[way][0],
        )

    def cot_start():
        for i in range(2):
            for way in range(2):
                go(cot_copy(way, (i + way) % 2, 0))

    def cot_step(i):
        s = i // 2
        for way in range(2):
            h = (i + way) % 2
            landed(cot.at[cot_slot(way, s + 1), hs[h]], cot_r.at[way, h, s])
            if i < 5:
                go(cot_copy(way, h, s + 1))

    def tg_part(i):
        e = (HERE + i) % NY
        part[e] = lax.dot_general(
            wts[...], cot[e], (((1,), (1,)), ((), ())), preferred_element_type=F32
        ).astype(BF16)
        for xl in range(2):
            src = part.at[e, pl.ds(pl.multiple_of((2 * xl + 1 - k) * own, 32), own)]
            go(remote(src, from_core.at[e, xl], gk_s.at[e, xl], gk_r.at[e, xl], core))

    def tg_x_copy(e, xl):
        there = 2 * (e % 2) + xl
        o = (x - there + NX) % NX
        slot = lax.max(o - 1, 0)
        return there != x, remote(
            summed.at[e, xl], from_x.at[e // 2, slot], gx_s.at[e, xl],
            gx_r.at[e // 2, slot], at(x=there),
        )

    def tg_sum(i):
        e = (HERE + i) % NY
        for xl in range(2):
            slot = from_core.at[e, xl]
            landed(slot, gk_r.at[e, xl])
            mine = part[e, pl.ds(pl.multiple_of((2 * xl + k) * own, 32), own)]
            summed[e, xl] = (mine.astype(F32) + slot[...].astype(F32)).astype(BF16)
            leaves, copy = tg_x_copy(e, xl)

            @pl.when(leaves)
            def _():
                copy.start()

    def tg_z_copy(j):
        o = (zh - j + NZ) % NZ
        slot = lax.max(o - 1, 0)
        return j != zh, remote(
            reduced.at[j], from_z.at[slot], gz_s.at[j], gz_r.at[slot], at(zh=j)
        )

    def tg_from_x(j):
        total = summed[2 * j + x // 2, x % 2].astype(F32)
        for o in range(NX - 1):
            landed(from_x.at[j, o], gx_r.at[j, o])
            total += from_x[j, o].astype(F32)
        reduced[j] = total.astype(BF16)
        leaves, copy = tg_z_copy(j)

        @pl.when(leaves)
        def _():
            copy.start()

    to_aft = remote(final, back, one_s.at[2], one_r.at[2], aft)
    to_home = remote(back, home, one_s.at[0], one_r.at[0], turn)

    def tg_from_z():
        total = reduced[zh].astype(F32)
        for o in range(NZ - 1):
            landed(from_z.at[o], gz_r.at[o])
            total += from_z[o].astype(F32)
        final[...] = total.astype(BF16)

        @pl.when(shifts)
        def _():
            to_aft.start()

    def tg_turn():
        @pl.when(shifts)
        def _():
            to_aft.wait_recv()

        @pl.when(jnp.logical_not(shifts))
        def _():
            back[...] = final[...]

        @pl.when(turns)
        def _():
            to_home.start()

    def tg_end():
        @pl.when(turns)
        def _():
            to_home.wait_recv()
            tgrad_ref[...] = home[...]

        @pl.when(jnp.logical_not(turns))
        def _():
            tgrad_ref[...] = back[...]

    def product(i):
        e = (HERE + i) % NY
        prod[e] = lax.dot_general(
            feats[e], wts[...], (((0,), (0,)), ((), ())), preferred_element_type=F32
        )

    def ring_copy(way, i):
        return remote(
            ring.at[way, i], ring.at[way, i + 2], ring_s.at[way, i], ring_r.at[way, i], ways[way][0]
        )

    def ring_goal(way, i):
        steps = (4 if i % 2 == 0 else 3) - i // 2
        return (HERE - ways[way][1] * steps + NY) % NY

    def ring_start(way, i):
        h = (i + way) % 2
        ring[way, i] = prod[ring_goal(way, i), hs[h]].astype(BF16)
        go(ring_copy(way, i))

    def ring_step(i):
        for way in range(2):
            h = (i + way) % 2
            slot = ring.at[way, i + 2]
            landed(slot, ring_r.at[way, i])
            if i < 5:
                slot[...] = (
                    slot[...].astype(F32) + prod[ring_goal(way, i + 2), hs[h]]
                ).astype(BF16)
                go(ring_copy(way, i + 2))

    def wg_half(which):
        total = jnp.zeros((rows, width), F32)
        for e in range(NY):
            total += jnp.dot(feats[e, which], cot[e], preferred_element_type=F32)
        return total

    wg_copy = remote(wg_send, wg_recv, one_s.at[3], one_r.at[3], pair)

    def wg_start():
        wg_send[...] = wg_half(other_rows).astype(BF16)
        go(wg_copy)

    def wg_own():
        wgrad_ref[...] = wg_half(own_rows)

    def wg_end():
        wg_copy.wait_recv()
        factor = columns(jnp.exp2(-expo[...].astype(F32)))
        for b in range(width // QBLOCK):
            cols = slice(b * QBLOCK, (b + 1) * QBLOCK)
            wgrad_ref[:, cols] = (
                wgrad_ref[:, cols] + wg_recv[:, cols].astype(F32)
            ) * factor[:, b : b + 1]

    def all_left():
        for copy in started:
            copy.wait_send()
        some = [tg_x_copy(e, xl) for e in range(NY) for xl in range(2)]
        some += [tg_z_copy(j) for j in range(NZ)]
        some += [(turns, copy) for copy in to_turn]
        some += [(shifts, copy) for copy in to_fore + [to_aft]]
        for leaves, copy in some:

            @pl.when(leaves)
            def _():
                copy.wait_send()

    loads[0].wait()
    tok_start()
    loads[1].wait()
    cot_start()
    weights_own()
    weights_send()
    loads[4].wait()
    tok_shift()
    cot_step(0)
    tok_own()
    cot_step(1)
    tok_from_z(1)
    cot_step(2)
    tok_from_z(2)
    weights_other()
    tg_part(0)
    tok_from_x(0)
    tg_part(1)
    tg_part(-1)
    cot_step(3)
    tok_from_x(1)
    tok_from_z(3)
    cot_step(4)
    tok_from_core(0)
    tok_from_core(1)
    product(4)
    ring_start(0, 0)
    ring_start(1, 0)
    product(-3)
    ring_start(1, 1)
    tg_sum(0)
    tg_sum(1)
    tg_sum(-1)
    tok_from_x(2)
    tok_from_core(7)
    product(3)
    ring_start(0, 1)
    tg_part(2)
    tg_part(-2)
    tg_sum(2)
    tg_sum(-2)
    cot_step(5)
    tg_part(3)
    tg_part(-3)
    tok_from_x(3)
    tg_sum(3)
    tg_sum(-3)
    cot_step(6)
    tg_part(4)
    tok_from_core(6)
    tok_from_core(2)
    tg_sum(4)
    product(2)
    product(-2)
    ring_step(0)
    tg_from_x(2)
    tok_from_core(5)
    tok_from_core(3)
    tok_from_core(4)
    wg_start()
    ring_step(1)
    tg_from_x(1)
    tg_from_x(3)
    product(1)
    product(-1)
    ring_step(2)
    product(0)
    tg_from_x(0)
    ring_step(3)
    ring_step(4)
    tg_from_z()
    wg_own()
    tg_turn()
    all_left()
    wg_end()
    ring_step(5)
    ring_step(6)
    for h in range(2):
        out_ref[hs[h]] = (
            prod[HERE, hs[h]]
            + ring[0, 8 - h].astype(F32)
            + ring[1, 7 + h].astype(F32)
        ).astype(BF16)

    tg_end()

    @pl.when(turns)
    def _():
        to_home.wait_send()


def on_device(tokens, weight_codes, weight_scales, cotangent, grad_exponents):
    count, own = tokens.shape
    rows, width = weight_codes.shape
    depth = 2 * rows
    dma = pltpu.SemaphoreType.DMA
    vmem = pl.BlockSpec(memory_space=pltpu.VMEM)
    scratch = [
        pltpu.VMEM((own, count), BF16),
        pltpu.VMEM((rows, width), jnp.int32),
        pltpu.VMEM((width // QBLOCK, rows), F32),
        pltpu.VMEM((width // QBLOCK, rows), jnp.int32),
        pltpu.VMEM((own, count), BF16),
        pltpu.VMEM((depth, width), BF16),
        pltpu.VMEM((NY, count, width), BF16),
        pltpu.VMEM((NY, depth, count), BF16),
        pltpu.VMEM((8, -(-rows // 128) * 128), F32),
        pltpu.VMEM((NY, depth, count), BF16),
        pltpu.VMEM((NY, 2, own, count), BF16),
        pltpu.VMEM((NY, 2, own, count), BF16),
        pltpu.VMEM((NZ, NX - 1, own, count), BF16),
        pltpu.VMEM((NZ, own, count), BF16),
        pltpu.VMEM((NZ - 1, own, count), BF16),
        pltpu.VMEM((own, count), BF16),
        pltpu.VMEM((own, count), BF16),
        pltpu.VMEM((own, count), BF16),
        pltpu.VMEM((NY, count, width), F32),
        pltpu.VMEM((2, 9, count // 2, width), BF16),
        pltpu.VMEM((rows, width), BF16),
        pltpu.VMEM((rows, width), BF16),
        dma((5,)),
        dma((PARTS,)), dma((PARTS,)),
        dma((PARTS,)), dma((PARTS,)),
        dma((2, 2, 4)), dma((2, 2, 4)),
        dma((4,)), dma((4,)),
        dma((NZ - 1, PARTS)), dma((NZ, PARTS)),
        dma((NZ, NX - 1, PARTS)), dma((NZ, NX - 1, PARTS)),
        dma((NY, 2)), dma((NY, 2)),
        dma((NY, 2)), dma((NY, 2)),
        dma((NY, 2)), dma((NZ, NX - 1)),
        dma((NZ,)), dma((NZ - 1,)),
        dma((2, 7)), dma((2, 7)),
    ]
    projected, token_grad, weight_grad = pl.pallas_call(
        kernel,
        name="up_projection",
        out_shape=(
            jax.ShapeDtypeStruct((count, width), BF16),
            jax.ShapeDtypeStruct((own, count), BF16),
            jax.ShapeDtypeStruct((rows, width), F32),
        ),
        in_specs=[pl.BlockSpec(memory_space=pltpu.HBM)] * 5,
        out_specs=(vmem, vmem, vmem),
        scratch_shapes=scratch,
        compiler_params=pltpu.CompilerParams(
            collective_id=0, has_side_effects=True, vmem_limit_bytes=VMEM
        ),
    )(tokens.T, weight_codes, weight_scales.T, cotangent, grad_exponents.T)
    return projected, token_grad.T, weight_grad


def solution(mesh):
    placed = P("node", "cross")
    return jax.shard_map(
        on_device,
        mesh=mesh,
        in_specs=(placed,) * 5,
        out_specs=(placed,) * 3,
        check_vma=False,
    )
```
